32 devices in a mesh: parts: 2 (over y), xy: 4 (over z), gz: 4 (over x, core).
Axes of the slice: x: 2, y: 2, z: 4, core: 2. Of those that a mesh axis runs over, the one named last changes fastest.
Arguments:
- features: bfloat16 [96, 65536], P(None, ('parts', 'xy', 'gz')), parts along dimension 1, may hold values from -6 to 6
- weight: bfloat16 [27, 96, 96], replicated, may hold values from -0.15625 to 0.15625
- z_send: int32 [8, 4, 512], P(('parts', 'xy'), 'gz'), parts along dimension 0, may hold values from -1 to 2047, as said below
- xy_send: int32 [8, 4, 1024], P(('parts', 'xy'), 'gz'), parts along dimension 0, may hold values from -1 to 2559, as said below
- kernel_map: int32 [27, 65536], P(None, ('parts', 'xy', 'gz')), parts along dimension 1, may hold values from -1 to 3583, as said below
- cotangent: bfloat16 [96, 65536], P(None, ('parts', 'xy', 'gz')), parts along dimension 1, may hold values from -6 to 6
Outputs:
- out_features: bfloat16 [96, 65536], P(None, ('parts', 'xy', 'gz')), parts along dimension 1
- grad_features: float32 [96, 65536], P(None, ('parts', 'xy', 'gz')), parts along dimension 1
- grad_weight: float32 [192, 2592], P(('parts', 'xy')), parts along dimension 0
The draws below stay inside these ranges and needn't reach their ends.
There are 2 independent parts, one for each index of `parts`. The reference program is written for one: setup_inputs(seed, part) draws one part's arguments, and reference() takes and returns one part's arrays. A program takes and returns all parts, laid end to end along the dimension named above; an argument that names none is the same for every part. Nothing has to cross between parts.
Inputs may be any that keep to these rules, and one draw needn't show every extreme that they name: `z_send`: slots of the device's own active voxels; the first 256 entries go to the layer below, the last 256 to the layer above; -1 marks an unused entry. `xy_send`: columns of the device's extended matrix; entries p * 256 to (p + 1) * 256 - 1 go to xy peer p; -1 marks an unused entry. `kernel_map`: column of the owning device's table; -1 where the offset has no active voxel or the slot is inactive; offset 27 // 2 of an active slot names that slot itself.
All inputs are finite; a program needn't handle non-finite values.
Results may differ from the reference program's by a relative error of at most 0.002.
Values may be sent and summed in bfloat16 or wider, within the bound.
A program may use at most 64 MiB of HBM per device.

```python
import math
import jax
import jax.numpy as jnp
from jax import lax

C = 96
K = 27
V_DEV = 2048
S_Z = 256
S_XY = 256
TABLE = 3584
NV = 32768
N_XY = 4
N_GZ = 4


def active_counts(key):
    device_total = N_XY * N_GZ
    counts = jax.random.randint(jax.random.fold_in(key, 7), (device_total,), V_DEV // 2, V_DEV + 1)
    return counts.at[0].set(V_DEV).astype(jnp.int32)


def draw_z_send(key, part):
    counts = active_counts(key)
    key = jax.random.fold_in(key, 11)
    key_pick, key_count = jax.random.split(key)
    device_total = N_XY * N_GZ
    raw_bits = jax.random.randint(key_pick, (device_total, 2, S_Z), 0, 1 << 30)
    picked = raw_bits % counts[:, None, None]
    used_count = jax.random.randint(key_count, (device_total, 2, 1), S_Z // 2, S_Z + 1)
    slot_index = jnp.arange(S_Z, dtype=jnp.int32)[None, None, :]
    layer = jnp.arange(device_total, dtype=jnp.int32) % N_GZ
    present = jnp.stack([layer > 0, layer < N_GZ - 1], axis=1)[:, :, None]
    lists = jnp.where((slot_index < used_count) & present, picked, -1)
    lists = lists.at[0, 1, 0].set(V_DEV - 1)
    return lists.reshape(N_XY, N_GZ, 2 * S_Z).astype(jnp.int32)


def draw_xy_send(key, part):
    counts = active_counts(key)
    key = jax.random.fold_in(key, 13)
    key_pick, key_count = jax.random.split(key)
    device_total = N_XY * N_GZ
    raw_bits = jax.random.randint(key_pick, (device_total, N_XY, S_XY), 0, 1 << 30)
    span = counts[:, None, None] + 2 * S_Z
    picked = raw_bits % span
    columns = jnp.where(picked < counts[:, None, None], picked, picked - counts[:, None, None] + V_DEV)
    used_count = jax.random.randint(key_count, (device_total, N_XY, 1), 0, S_XY + 1)
    slot_index = jnp.arange(S_XY, dtype=jnp.int32)[None, None, :]
    lists = jnp.where(slot_index < used_count, columns, -1)
    lists = lists.at[0, 0, 0].set(V_DEV + 2 * S_Z - 1)
    return lists.reshape(N_XY, N_GZ, N_XY * S_XY).astype(jnp.int32)


def draw_kernel_map(key, part):
    counts = active_counts(key)
    key = jax.random.fold_in(key, 17)
    key_live, key_where, key_pick = jax.random.split(key, 3)
    column = jnp.arange(NV, dtype=jnp.int32)
    device = column // V_DEV
    slot_index = column % V_DEV
    device_count = counts[device]
    active = slot_index < device_count
    live = jax.random.randint(key_live, (K, NV), 0, 8) < 5
    local = jax.random.randint(key_where, (K, NV), 0, 4) != 0
    raw_bits = jax.random.randint(key_pick, (K, NV), 0, 1 << 30)
    own_pick = raw_bits % device_count[None, :]
    halo_pick = V_DEV + raw_bits % (TABLE - V_DEV)
    target = jnp.where(local, own_pick, halo_pick)
    target = jnp.where(live, target, -1)
    centre = jnp.arange(K, dtype=jnp.int32)[:, None] == K // 2
    target = jnp.where(centre, slot_index[None, :], target)
    target = jnp.where(active[None, :], target, -1)
    target = target.at[0, 0].set(TABLE - 1).at[1, 0].set(-1)
    return target.astype(jnp.int32)


def spiked(values, rng, source, target, shards_of, factor):
    def block_of(position):
        return (jnp.arange(values.shape[position]) // (values.shape[position] // shards_of)).reshape((-1,) + (1,) * (values.ndim - 1 - position))

    near = jax.random.permutation(rng, shards_of)[block_of(target)]
    other_side = (block_of(target) + shards_of // 2) % shards_of
    return jnp.where((block_of(source) == near) | (block_of(source) == other_side), factor * values, values)


def block_scale(own_key, dims, shards, least, largest):
    level = 1.0
    for axis_at, parts in shards:
        draws = jax.random.uniform(jax.random.fold_in(jax.random.fold_in(own_key, 6), axis_at), (parts,), jnp.float32, least / len(shards), largest / len(shards))
        level = level * jnp.repeat(jnp.exp(draws), dims[axis_at] // parts).reshape((-1,) + (1,) * (len(dims) - 1 - axis_at))
    return level


def scatter_about(stream_key, dims, deviation, limit, pieces=(), kind=jnp.bfloat16):
    values = jax.random.normal(stream_key, dims, jnp.float32) * deviation
    if len(pieces) > 0:
        values = block_scale(stream_key, dims, pieces, -0.22, 0.18) * values
    return jnp.clip(values, min=-limit, max=limit).astype(kind)


def gaussian_with(stream_key, dims, spread, bound, shards, heavy, held_as=jnp.bfloat16):
    drawn = spread * jax.random.normal(stream_key, dims, jnp.float32)
    if shards:
        drawn = drawn * block_scale(stream_key, dims, shards, -0.22, 0.18)
    return jnp.clip(spiked(drawn, jax.random.fold_in(stream_key, 3), *heavy), -bound, bound).astype(held_as)


def setup_inputs(seed: int = 0, part: int = 0) -> dict:
    arg_keys = jax.random.split(jax.random.key(seed), 7)
    own_keys = jax.random.split(jax.random.fold_in(arg_keys[6], part), 7)
    features = scatter_about(own_keys[0], (C, NV), 1.0, 6.0, ((1, 16),))
    weight = scatter_about(arg_keys[1], (K, C, C), (K * C // 2) ** -0.5, 0.15625)
    z_send = draw_z_send(jax.random.fold_in(jax.random.fold_in(arg_keys[6], part), 71), part)
    xy_send = draw_xy_send(jax.random.fold_in(jax.random.fold_in(arg_keys[6], part), 71), part)
    kernel_map = draw_kernel_map(jax.random.fold_in(jax.random.fold_in(arg_keys[6], part), 71), part)
    cotangent = gaussian_with(own_keys[5], (C, NV), 1.0, 6.0, ((1, 16),), (1, 0, 16, 2.0))
    return {"features": features, "weight": weight, "z_send": z_send, "xy_send": xy_send, "kernel_map": kernel_map, "cotangent": cotangent}


def pick_columns(voxel_table, col_index):
    table_width = voxel_table.shape[1]
    padded = jnp.concatenate([voxel_table, jnp.zeros((voxel_table.shape[0], 1), voxel_table.dtype)], axis=1)
    safe_index = jnp.where(col_index < 0, table_width, col_index).astype(jnp.int32)
    return jnp.take(padded, safe_index, axis=1)

def add_columns(base_grad, col_index, values):
    table_width = base_grad.shape[1]
    padded = jnp.concatenate([base_grad, jnp.zeros((base_grad.shape[0], 1), base_grad.dtype)], axis=1)
    safe_index = jnp.where(col_index < 0, table_width, col_index).astype(jnp.int32)
    return padded.at[:, safe_index].add(values.astype(base_grad.dtype))[:, :table_width]

def device_pass(voxel_table, index_map, upstream, weight):
    channels, slots = upstream.shape
    upstream_wide = upstream.astype(jnp.float32)

    def offset_step(loop_state, inputs):
        out_sum, grad_table = loop_state
        w_offset, col_index = inputs
        w_wide = w_offset.astype(jnp.float32)
        columns = pick_columns(voxel_table, col_index).astype(jnp.float32)
        out_sum = out_sum + jnp.dot(w_wide.T, columns, preferred_element_type=jnp.float32)
        back_grad = jnp.dot(w_wide, upstream_wide, preferred_element_type=jnp.float32)
        grad_table = add_columns(grad_table, col_index, back_grad)
        w_piece = jnp.dot(upstream_wide, columns.T, preferred_element_type=jnp.float32)
        return ((out_sum, grad_table), w_piece)
    start_state = (jnp.zeros((channels, slots), jnp.float32), jnp.zeros(voxel_table.shape, jnp.float32))
    (out_sum, grad_table), w_pieces = lax.scan(offset_step, start_state, (weight, index_map))
    return (out_sum, grad_table, w_pieces)

def reference(features, weight, z_send, xy_send, kernel_map, cotangent):
    device_total = N_XY * N_GZ
    own = features.reshape(C, N_XY, N_GZ, V_DEV).transpose(1, 2, 0, 3)
    pick_all = jax.vmap(jax.vmap(pick_columns))
    add_all = jax.vmap(jax.vmap(add_columns))
    outgoing = pick_all(own, z_send)
    zero_rim = jnp.zeros((N_XY, 1, C, S_Z), features.dtype)
    from_below = jnp.concatenate([zero_rim, outgoing[:, :-1, :, S_Z:]], axis=1)
    from_above = jnp.concatenate([outgoing[:, 1:, :, :S_Z], zero_rim], axis=1)
    extended = jnp.concatenate([own, from_below, from_above], axis=3)
    send_blocks = pick_all(extended, xy_send).reshape(N_XY, N_GZ, C, N_XY, S_XY)
    received = send_blocks.transpose(3, 1, 2, 0, 4).reshape(N_XY, N_GZ, C, N_XY * S_XY)
    voxel_table = jnp.concatenate([extended, received], axis=3)
    tables = voxel_table.reshape(device_total, C, TABLE)
    index_maps = kernel_map.reshape(K, device_total, V_DEV).transpose(1, 0, 2)
    upstreams = cotangent.reshape(C, device_total, V_DEV).transpose(1, 0, 2)

    def device_step(w_total, inputs):
        table_one, map_one, upstream_one = inputs
        out_sum, grad_table, w_pieces = device_pass(table_one, map_one, upstream_one, weight)
        return (w_total + w_pieces, (out_sum.astype(jnp.bfloat16), grad_table))
    w_total, (out_blocks, grad_tables) = lax.scan(device_step, jnp.zeros((K, C, C), jnp.float32), (tables, index_maps, upstreams))
    out_features = out_blocks.transpose(1, 0, 2).reshape(C, NV)
    grad_tables = grad_tables.reshape(N_XY, N_GZ, C, TABLE)
    ext_width = V_DEV + 2 * S_Z
    grad_recv = grad_tables[..., ext_width:].reshape(N_XY, N_GZ, C, N_XY, S_XY)
    returned = grad_recv.transpose(3, 1, 2, 0, 4).reshape(N_XY, N_GZ, C, N_XY * S_XY)
    grad_ext = add_all(grad_tables[..., :ext_width], xy_send, returned)
    grad_below = grad_ext[..., V_DEV:V_DEV + S_Z]
    grad_above = grad_ext[..., V_DEV + S_Z:]
    zero_grad = jnp.zeros((N_XY, 1, C, S_Z), jnp.float32)
    to_lower = jnp.concatenate([zero_grad, grad_above[:, :-1]], axis=1)
    to_upper = jnp.concatenate([grad_below[:, 1:], zero_grad], axis=1)
    grad_outgoing = jnp.concatenate([to_lower, to_upper], axis=3)
    grad_own = add_all(grad_ext[..., :V_DEV], z_send, grad_outgoing)
    grad_features = grad_own.transpose(2, 0, 1, 3).reshape(C, NV)
    w_scale = 1.0 / math.sqrt(NV)
    grad_weight = w_total.transpose(1, 0, 2).reshape(C, K * C) * w_scale
    return (out_features, grad_features, grad_weight)
```

```python
import functools
import math

import jax
import jax.numpy as jnp
from jax import lax
from jax.experimental import pallas as pl
from jax.experimental.pallas import tpu as pltpu
from jax.sharding import PartitionSpec as P

LO = 256
BF = jnp.bfloat16
F32 = jnp.float32
VMEM_LIMIT = 56 * 1024 * 1024


def split_index(index):
    return index >> 8, index & (LO - 1)


def one_hot(lo):
    rows = lax.broadcasted_iota(jnp.int32, (LO, lo.shape[1]), 0)
    return jnp.where(rows == lo, 1.0, 0.0).astype(BF)


def pick(blocks, index):
    count, channels, _ = blocks.shape
    hi, lo = split_index(index)
    found = jnp.dot(
        blocks.reshape(count * channels, LO), one_hot(lo), preferred_element_type=F32
    ).reshape(count, channels, index.shape[1])
    got = jnp.zeros((channels, index.shape[1]), F32)
    for h in range(count):
        got = jnp.where(hi == h, found[h], got)
    return got.astype(BF)


def spread(values, index, first, count):
    channels, width = values.shape
    hi, lo = split_index(index)
    parts = [values * jnp.where(hi == first + h, 1.0, 0.0).astype(BF) for h in range(count)]
    wide = jnp.concatenate(parts, axis=0)
    added = lax.dot_general(
        wide, one_hot(lo), (((1,), (1,)), ((), ())), preferred_element_type=F32
    )
    return added.reshape(count, channels, LO)


def whole(array_or_shape):
    shape = array_or_shape.shape
    return pl.BlockSpec(shape, lambda *_: (0,) * len(shape))


def params():
    return pltpu.CompilerParams(vmem_limit_bytes=VMEM_LIMIT)


def fill_blocks(blocks, own_ref, *rest):
    count = own_ref.shape[1] // LO
    for h in range(count):
        blocks[h] = own_ref[:, h * LO : (h + 1) * LO]
    at = count
    for ref in rest:
        blocks[at : at + ref.shape[0]] = ref[...]
        at += ref.shape[0]


def pick_kernel(*refs):
    index_ref, out_ref, blocks = refs[-3], refs[-2], refs[-1]
    fill_blocks(blocks, *refs[:-3])
    for b in range(out_ref.shape[0]):
        out_ref[b] = pick(blocks[...], index_ref[:, b * LO : (b + 1) * LO])


def pick_blocks(own, rest, index):
    channels, slots = own.shape
    width = index.shape[0]
    count = slots // LO + sum(r.shape[0] for r in rest)
    return pl.pallas_call(
        pick_kernel,
        out_shape=jax.ShapeDtypeStruct((width // LO, channels, LO), BF),
        scratch_shapes=[pltpu.VMEM((count, channels, LO), BF)],
        compiler_params=params(),
        name="pick_columns",
    )(own, *rest, index.reshape(1, width))


def conv_kernel(chunk, own_ref, z_ref, xy_ref, wt_ref, index_ref, up_ref, out_ref, wg_ref, blocks, got):
    k = pl.program_id(0)
    channels, slots = own_ref.shape

    @pl.when(k == 0)
    def _():
        fill_blocks(blocks, own_ref, z_ref, xy_ref)

    rows = pl.ds(pl.multiple_of(k * channels, 32), channels)

    @pl.loop(0, slots // chunk)
    def _(j):
        cols = pl.ds(pl.multiple_of(j * chunk, chunk), chunk)
        got[rows, cols] = pick(blocks[...], index_ref[0, :, cols])

    @pl.when(k == pl.num_programs(0) - 1)
    def _():
        @pl.loop(0, slots // LO)
        def _(j):
            cols = pl.ds(pl.multiple_of(j * LO, LO), LO)
            out_ref[:, cols] = jnp.dot(
                wt_ref[...], got[:, cols], preferred_element_type=F32
            ).astype(BF)

        @pl.loop(0, got.shape[0] // (3 * channels))
        def _(j):
            part = pl.ds(pl.multiple_of(j * 3 * channels, 32), 3 * channels)
            wg_ref[part, :] = lax.dot_general(
                got[part, :], up_ref[...], (((1,), (1,)), ((), ())), preferred_element_type=F32
            )


def convolve(own, z_blocks, xy_blocks, weight_t, index, up, chunk=512):
    channels, slots = own.shape
    offsets = index.shape[0]
    count = slots // LO + z_blocks.shape[0] + xy_blocks.shape[0]
    flops = 2 * offsets * slots * channels * (count * LO + 2 * channels)
    return pl.pallas_call(
        functools.partial(conv_kernel, chunk),
        grid=(offsets,),
        in_specs=[
            whole(own),
            whole(z_blocks),
            whole(xy_blocks),
            whole(weight_t),
            pl.BlockSpec((1, 1, slots), lambda k: (k, 0, 0)),
            whole(up),
        ],
        out_specs=[
            pl.BlockSpec((channels, slots), lambda k: (0, 0)),
            pl.BlockSpec((offsets * channels, channels), lambda k: (0, 0)),
        ],
        out_shape=[
            jax.ShapeDtypeStruct((channels, slots), BF),
            jax.ShapeDtypeStruct((offsets * channels, channels), F32),
        ],
        scratch_shapes=[
            pltpu.VMEM((count, channels, LO), BF),
            pltpu.VMEM((offsets * channels, slots), BF),
        ],
        compiler_params=params(),
        cost_estimate=pl.CostEstimate(flops=flops, bytes_accessed=4 << 20, transcendentals=0),
        name="convolve",
    )(own, z_blocks, xy_blocks, weight_t, index, up)


def spread_kernel(first, chunk, w_ref, index_ref, up_ref, acc_ref):
    @pl.when(pl.program_id(0) == 0)
    def _():
        acc_ref[...] = jnp.zeros_like(acc_ref)

    @pl.loop(0, up_ref.shape[1] // chunk)
    def _(j):
        cols = pl.ds(pl.multiple_of(j * chunk, chunk), chunk)
        back = jnp.dot(w_ref[0], up_ref[:, cols], preferred_element_type=F32).astype(BF)
        acc_ref[...] += spread(back, index_ref[0, :, cols], first, acc_ref.shape[0])


def spread_grads(weight, index, up, first, count, chunk=1024):
    channels, slots = up.shape
    offsets = index.shape[0]
    flops = 2 * offsets * slots * channels * (count * LO + channels)
    return pl.pallas_call(
        functools.partial(spread_kernel, first, chunk),
        grid=(offsets,),
        in_specs=[
            pl.BlockSpec((1, channels, channels), lambda k: (k, 0, 0)),
            pl.BlockSpec((1, 1, slots), lambda k: (k, 0, 0)),
            whole(up),
        ],
        out_specs=pl.BlockSpec((count, channels, LO), lambda k: (0, 0, 0)),
        out_shape=jax.ShapeDtypeStruct((count, channels, LO), F32),
        compiler_params=params(),
        cost_estimate=pl.CostEstimate(flops=flops, bytes_accessed=2 << 20, transcendentals=0),
        name="spread_grads",
    )(weight, index, up)


def add_kernel(blocks_ref, index_ref, out_ref):
    for b in range(blocks_ref.shape[0]):
        part = spread(blocks_ref[b], index_ref[:, b * LO : (b + 1) * LO], 0, out_ref.shape[0])
        if b == 0:
            out_ref[...] = part
        else:
            out_ref[...] += part


def add_blocks(blocks, index, count):
    _, channels, _ = blocks.shape
    return pl.pallas_call(
        add_kernel,
        out_shape=jax.ShapeDtypeStruct((count, channels, LO), F32),
        compiler_params=params(),
        name="add_columns",
    )(blocks, index.reshape(1, -1))


def last_kernel(own_ref, ext_ref, blocks_ref, index_ref, out_ref):
    count = own_ref.shape[0]
    total = own_ref[...] + ext_ref[...]
    for b in range(blocks_ref.shape[0]):
        total += spread(blocks_ref[b], index_ref[:, b * LO : (b + 1) * LO], 0, count)
    for h in range(count):
        out_ref[:, h * LO : (h + 1) * LO] = total[h]


def last_add(own, ext, blocks, index):
    count, channels, _ = own.shape
    return pl.pallas_call(
        last_kernel,
        grid=(1,),
        in_specs=[
            whole(own),
            pl.BlockSpec(own.shape, lambda i: (0, 0, 0)),
            whole(blocks),
            pl.BlockSpec((1, index.shape[0]), lambda i: (0, 0)),
        ],
        out_specs=pl.BlockSpec((channels, count * LO), lambda i: (0, 0)),
        out_shape=jax.ShapeDtypeStruct((channels, count * LO), F32),
        compiler_params=params(),
        name="last_add",
    )(own, ext, blocks, index.reshape(1, -1))


def exchange(blocks, peers, per_peer):
    count, channels, _ = blocks.shape
    if per_peer != LO:
        flat = blocks.transpose(1, 0, 2).reshape(channels, peers, per_peer).transpose(1, 0, 2)
    else:
        flat = blocks
    got = lax.all_to_all(flat, "xy", split_axis=0, concat_axis=0, tiled=True)
    if per_peer != LO:
        got = got.transpose(1, 0, 2).reshape(channels, count, LO).transpose(1, 0, 2)
    return got


def shift_z(low_bound, high_bound):
    count = lax.axis_size("gz")
    up = [(i, i + 1) for i in range(count - 1)]
    down = [(b, a) for a, b in up]
    return lax.ppermute(high_bound, "gz", up), lax.ppermute(low_bound, "gz", down)


def on_device(features, weight, z_send, xy_send, kernel_map, cotangent):
    channels, slots = features.shape
    offsets = weight.shape[0]
    peers = lax.axis_size("xy")
    z_list, xy_list = z_send.reshape(-1), xy_send.reshape(-1)
    z_count = z_list.shape[0] // LO
    rim = z_count // 2
    xy_count = xy_list.shape[0] // LO
    per_peer = xy_list.shape[0] // peers
    own_count = slots // LO
    ext_count = own_count + z_count
    index = kernel_map.reshape(offsets, 1, slots)

    outgoing = pick_blocks(features, (), z_list)
    below, above = shift_z(outgoing[:rim], outgoing[rim:])
    z_blocks = jnp.concatenate([below, above], axis=0)

    halo_grad = spread_grads(weight, index, cotangent, own_count, z_count + xy_count)

    sends = pick_blocks(features, (z_blocks,), xy_list)
    xy_blocks = exchange(sends, peers, per_peer)
    returned = exchange(halo_grad[z_count:].astype(BF), peers, per_peer)
    ext_grad = add_blocks(returned, xy_list, ext_count)
    z_grad = (halo_grad[:z_count] + ext_grad[own_count:]).astype(BF)
    back_low, back_high = shift_z(z_grad[:rim], z_grad[rim:])
    z_back = jnp.concatenate([back_low, back_high], axis=0)

    weight_t = weight.transpose(2, 0, 1).reshape(channels, offsets * channels)
    out_features, w_term = convolve(features, z_blocks, xy_blocks, weight_t, index, cotangent)
    w_scale = 1.0 / math.sqrt(slots * peers * lax.axis_size("gz"))
    w_mine = lax.psum_scatter(w_term.T, "xy", scatter_dimension=0, tiled=True)
    grad_weight = lax.psum(w_mine, "gz") * w_scale

    own_grad = spread_grads(weight, index, cotangent, 0, own_count)
    grad_features = last_add(own_grad, ext_grad, z_back, z_list)
    return (out_features, grad_features, grad_weight)


def solution(mesh):
    slab = P(None, ("parts", "xy", "gz"))
    lists = P(("parts", "xy"), "gz", None)
    return jax.shard_map(
        on_device,
        mesh=mesh,
        in_specs=(slab, P(), lists, lists, slab, slab),
        out_specs=(slab, slab, P(("parts", "xy"), None)),
        check_vma=False,
    )
```

```python
import functools
import math

import jax
import jax.numpy as jnp
from jax import lax
from jax.experimental import pallas as pl
from jax.experimental.pallas import tpu as pltpu
from jax.sharding import PartitionSpec as P

LO = 256
BF = jnp.bfloat16
F32 = jnp.float32
VMEM_LIMIT = 56 * 1024 * 1024


def split_index(index):
    return index >> 8, index & (LO - 1)


def one_hot(lo):
    rows = lax.broadcasted_iota(jnp.int32, (LO, lo.shape[1]), 0)
    return jnp.where(rows == lo, 1.0, 0.0).astype(BF)


def pick(blocks, index):
    count, channels, _ = blocks.shape
    hi, lo = split_index(index)
    found = jnp.dot(
        blocks.reshape(count * channels, LO), one_hot(lo), preferred_element_type=F32
    ).reshape(count, channels, index.shape[1])
    got = jnp.zeros((channels, index.shape[1]), F32)
    for h in range(count):
        got = jnp.where(hi == h, found[h], got)
    return got.astype(BF)


def spread(values, index, first, count):
    channels, width = values.shape
    hi, lo = split_index(index)
    parts = [values * jnp.where(hi == first + h, 1.0, 0.0).astype(BF) for h in range(count)]
    wide = jnp.concatenate(parts, axis=0)
    added = lax.dot_general(
        wide, one_hot(lo), (((1,), (1,)), ((), ())), preferred_element_type=F32
    )
    return added.reshape(count, channels, LO)


def whole(array_or_shape):
    shape = array_or_shape.shape
    return pl.BlockSpec(shape, lambda *_: (0,) * len(shape))


def params():
    return pltpu.CompilerParams(vmem_limit_bytes=VMEM_LIMIT)


def fill_blocks(blocks, own_ref, *rest):
    count = own_ref.shape[1] // LO
    for h in range(count):
        blocks[h] = own_ref[:, h * LO : (h + 1) * LO]
    at = count
    for ref in rest:
        blocks[at : at + ref.shape[0]] = ref[...]
        at += ref.shape[0]


def pick_kernel(*refs):
    index_ref, out_ref, blocks = refs[-3], refs[-2], refs[-1]
    fill_blocks(blocks, *refs[:-3])
    for b in range(out_ref.shape[0]):
        out_ref[b] = pick(blocks[...], index_ref[:, b * LO : (b + 1) * LO])


def pick_blocks(own, rest, index):
    channels, slots = own.shape
    width = index.shape[0]
    count = slots // LO + sum(r.shape[0] for r in rest)
    return pl.pallas_call(
        pick_kernel,
        out_shape=jax.ShapeDtypeStruct((width // LO, channels, LO), BF),
        scratch_shapes=[pltpu.VMEM((count, channels, LO), BF)],
        compiler_params=params(),
        name="pick_columns",
    )(own, *rest, index.reshape(1, width))


def conv_kernel(own_ref, z_ref, xy_ref, wt_ref, index_ref, up_ref, out_ref, wg_ref, blocks, got):
    k = pl.program_id(0)
    channels, slots = own_ref.shape

    @pl.when(k == 0)
    def _():
        fill_blocks(blocks, own_ref, z_ref, xy_ref)

    rows = pl.ds(pl.multiple_of(k * channels, 32), channels)
    got[rows, :] = pick(blocks[...], index_ref[0])

    @pl.when(k == pl.num_programs(0) - 1)
    def _():
        out_ref[...] = jnp.dot(wt_ref[...], got[...], preferred_element_type=F32).astype(BF)
        wg_ref[...] = lax.dot_general(
            up_ref[...], got[...], (((1,), (1,)), ((), ())), preferred_element_type=F32
        )


def convolve(own, z_blocks, xy_blocks, weight_t, index, up):
    channels, slots = own.shape
    offsets = index.shape[0]
    count = slots // LO + z_blocks.shape[0] + xy_blocks.shape[0]
    flops = 2 * offsets * slots * channels * (count * LO + 2 * channels)
    return pl.pallas_call(
        conv_kernel,
        grid=(offsets,),
        in_specs=[
            whole(own),
            whole(z_blocks),
            whole(xy_blocks),
            whole(weight_t),
            pl.BlockSpec((1, 1, slots), lambda k: (k, 0, 0)),
            whole(up),
        ],
        out_specs=[
            pl.BlockSpec((channels, slots), lambda k: (0, 0)),
            pl.BlockSpec((channels, offsets * channels), lambda k: (0, 0)),
        ],
        out_shape=[
            jax.ShapeDtypeStruct((channels, slots), BF),
            jax.ShapeDtypeStruct((channels, offsets * channels), F32),
        ],
        scratch_shapes=[
            pltpu.VMEM((count, channels, LO), BF),
            pltpu.VMEM((offsets * channels, slots), BF),
        ],
        compiler_params=params(),
        cost_estimate=pl.CostEstimate(flops=flops, bytes_accessed=4 << 20, transcendentals=0),
        name="convolve",
    )(own, z_blocks, xy_blocks, weight_t, index, up)


def spread_step(w_ref, index_ref, up_ref, back, first, count):
    k = pl.program_id(0)
    channels = up_ref.shape[0]

    @pl.when(k == 0)
    def _():
        back[...] = jnp.dot(w_ref[...], up_ref[...], preferred_element_type=F32).astype(BF)

    rows = pl.ds(pl.multiple_of(k * channels, 32), channels)
    return spread(back[rows, :], index_ref[0], first, count)


def spread_kernel(first, w_ref, index_ref, up_ref, *refs):
    acc_ref, back = refs[-2:]
    part = spread_step(w_ref, index_ref, up_ref, back, first, acc_ref.shape[0])

    @pl.when(pl.program_id(0) == 0)
    def _():
        acc_ref[...] = part + refs[0][...] if len(refs) == 3 else part

    @pl.when(pl.program_id(0) > 0)
    def _():
        acc_ref[...] += part


def spread_last_kernel(
    w_ref, index_ref, up_ref, start_ref, ext_ref, z_ref, z_index_ref, out_ref, back, acc
):
    count = acc.shape[0]

    @pl.when(pl.program_id(0) == 0)
    def _():
        acc[...] = start_ref[...] + ext_ref[...] + spread_pairs(z_ref, z_index_ref, count)

    acc[...] += spread_step(w_ref, index_ref, up_ref, back, 0, count)

    @pl.when(pl.program_id(0) == pl.num_programs(0) - 1)
    def _():
        for h in range(count):
            out_ref[:, h * LO : (h + 1) * LO] = acc[h]


def spread_specs(weight, up, begin, end):
    channels, slots = up.shape
    steps = end - begin
    return [
        pl.BlockSpec((steps * channels, channels), lambda k: (0, 0)),
        pl.BlockSpec((1, 1, slots), lambda k: (k + begin, 0, 0)),
        whole(up),
    ]


def spread_cost(up, count, steps):
    channels, slots = up.shape
    flops = 2 * steps * slots * channels * (count * LO + channels)
    return pl.CostEstimate(flops=flops, bytes_accessed=2 << 20, transcendentals=0)


def weight_rows(weight, begin, end):
    return weight[begin:end].reshape(-1, weight.shape[2])


def spread_grads(weight, index, up, first, count, begin, end, start=None):
    channels, slots = up.shape
    extra = () if start is None else (start,)
    steps = end - begin
    return pl.pallas_call(
        functools.partial(spread_kernel, first),
        grid=(steps,),
        in_specs=spread_specs(weight, up, begin, end) + [whole(e) for e in extra],
        out_specs=pl.BlockSpec((count, channels, LO), lambda k: (0, 0, 0)),
        out_shape=jax.ShapeDtypeStruct((count, channels, LO), F32),
        scratch_shapes=[pltpu.VMEM((steps * channels, slots), BF)],
        compiler_params=params(),
        cost_estimate=spread_cost(up, count, steps),
        name="spread_grads",
    )(weight_rows(weight, begin, end), index, up, *extra)


def spread_last(weight, index, up, begin, end, start, ext, z_pairs, z_index):
    count, channels, _ = start.shape
    slots = up.shape[1]
    steps = end - begin
    return pl.pallas_call(
        spread_last_kernel,
        grid=(steps,),
        in_specs=spread_specs(weight, up, begin, end)
        + [
            whole(start),
            pl.BlockSpec(start.shape, lambda k: (0, 0, 0)),
            whole(z_pairs),
            pl.BlockSpec((1, z_index.shape[0]), lambda k: (0, 0)),
        ],
        out_specs=pl.BlockSpec((channels, slots), lambda k: (0, 0)),
        out_shape=jax.ShapeDtypeStruct((channels, slots), F32),
        scratch_shapes=[
            pltpu.VMEM((steps * channels, slots), BF),
            pltpu.VMEM((count, channels, LO), F32),
        ],
        compiler_params=params(),
        cost_estimate=spread_cost(up, count, steps),
        name="spread_last",
    )(weight_rows(weight, begin, end), index, up, start, ext, z_pairs, z_index.reshape(1, -1))


def split_pair(value):
    high = value.astype(BF)
    low = (value - high.astype(F32)).astype(BF)
    return jnp.concatenate([high, low], axis=1)


def spread_pairs(pairs_ref, index_ref, count):
    channels = pairs_ref.shape[1] // 2
    index = jnp.concatenate([index_ref[...], index_ref[...]], axis=1)
    blocks = range(pairs_ref.shape[0])
    values = [pairs_ref[b, :channels, :] for b in blocks] + [
        pairs_ref[b, channels:, :] for b in blocks
    ]
    return spread(jnp.concatenate(values, axis=1), index, 0, count)


def halo_add_kernel(slots, pairs_ref, index_ref, halo_ref, ext_ref, z_ref):
    own_count = slots // LO
    z_count, channels, _ = z_ref.shape[0], ext_ref.shape[1], LO
    part = spread_pairs(pairs_ref, index_ref, own_count + z_count)
    ext_ref[...] = part[:own_count]
    z_ref[...] = split_pair(part[own_count:] + halo_ref[:z_count])


def halo_add(pairs, index, halo, own_count, z_count):
    channels = halo.shape[1]
    return pl.pallas_call(
        functools.partial(halo_add_kernel, own_count * LO),
        out_shape=[
            jax.ShapeDtypeStruct((own_count, channels, LO), F32),
            jax.ShapeDtypeStruct((z_count, 2 * channels, LO), BF),
        ],
        compiler_params=params(),
        name="halo_add",
    )(pairs, index.reshape(1, -1), halo)


def exchange(blocks, peers, per_peer):
    count, channels, _ = blocks.shape
    if per_peer != LO:
        flat = blocks.transpose(1, 0, 2).reshape(channels, peers, per_peer).transpose(1, 0, 2)
    else:
        flat = blocks
    got = lax.all_to_all(flat, "xy", split_axis=0, concat_axis=0, tiled=True)
    if per_peer != LO:
        got = got.transpose(1, 0, 2).reshape(channels, count, LO).transpose(1, 0, 2)
    return got


def shift_z(low_bound, high_bound):
    count = lax.axis_size("gz")
    up = [(i, i + 1) for i in range(count - 1)]
    down = [(b, a) for a, b in up]
    return lax.ppermute(high_bound, "gz", up), lax.ppermute(low_bound, "gz", down)


def on_device(features, weight, z_send, xy_send, kernel_map, cotangent):
    channels, slots = features.shape
    offsets = weight.shape[0]
    peers = lax.axis_size("xy")
    z_list, xy_list = z_send.reshape(-1), xy_send.reshape(-1)
    z_count = z_list.shape[0] // LO
    rim = z_count // 2
    xy_count = xy_list.shape[0] // LO
    per_peer = xy_list.shape[0] // peers
    own_count = slots // LO
    ext_count = own_count + z_count
    index = kernel_map.reshape(offsets, 1, slots)

    outgoing = pick_blocks(features, (), z_list)
    below, above = shift_z(outgoing[:rim], outgoing[rim:])
    z_blocks = jnp.concatenate([below, above], axis=0)

    cotangent, outgoing = lax.optimization_barrier((cotangent, outgoing))
    halo_grad = spread_grads(
        weight, index, cotangent, own_count, z_count + xy_count, 0, offsets
    )
    z_blocks, halo_grad = lax.optimization_barrier((z_blocks, halo_grad))

    sends = pick_blocks(features, (z_blocks,), xy_list)
    both = jnp.concatenate([sends, split_pair(halo_grad[z_count:])], axis=1)
    got = exchange(both, peers, per_peer)
    own_grad = spread_grads(weight, index, cotangent, 0, own_count, 0, offsets // 3)

    xy_blocks, xy_pairs = got[:, :channels], got[:, channels:]
    ext_grad, z_pairs = halo_add(xy_pairs, xy_list, halo_grad, own_count, z_count)
    back_low, back_high = shift_z(z_pairs[:rim], z_pairs[rim:])
    z_back = jnp.concatenate([back_low, back_high], axis=0)

    weight_t = weight.transpose(2, 0, 1).reshape(channels, offsets * channels)
    xy_blocks, own_grad = lax.optimization_barrier((xy_blocks, own_grad))
    out_features, w_term = convolve(features, z_blocks, xy_blocks, weight_t, index, cotangent)

    layers = lax.axis_size("gz")
    w_scale = 1.0 / math.sqrt(slots * peers * layers)
    cotangent, w_term = lax.optimization_barrier((cotangent, w_term))
    middle = 2 * offsets // 3
    own_grad = spread_grads(
        weight, index, cotangent, 0, own_count, offsets // 3, middle, start=own_grad
    )
    if channels % (peers * layers) == 0:
        rows = channels // (peers * layers)
        terms = lax.all_to_all(
            w_term.reshape(peers * layers, rows, -1), ("xy", "gz"), 0, 0, tiled=True
        )
        own_grad, terms = lax.optimization_barrier((own_grad, terms))
        mine = jnp.sum(terms, axis=0) * w_scale
        grad_weight = lax.all_gather(mine, "gz", axis=0, tiled=True)
    else:
        part = lax.psum_scatter(w_term, "xy", scatter_dimension=0, tiled=True)
        grad_weight = lax.psum(part, "gz") * w_scale
    grad_features = spread_last(
        weight, index, cotangent, middle, offsets, own_grad, ext_grad, z_back, z_list
    )
    return (out_features, grad_features, grad_weight)


def solution(mesh):
    slab = P(None, ("parts", "xy", "gz"))
    lists = P(("parts", "xy"), "gz", None)
    return jax.shard_map(
        on_device,
        mesh=mesh,
        in_specs=(slab, P(), lists, lists, slab, slab),
        out_specs=(slab, slab, P(("parts", "xy"), None)),
        check_vma=False,
    )
```

```python
import functools
import math

import jax
import jax.numpy as jnp
from jax import lax
from jax.experimental import pallas as pl
from jax.experimental.pallas import tpu as pltpu
from jax.sharding import PartitionSpec as P

LO = 256
BF = jnp.bfloat16
F32 = jnp.float32
GROUP = 3
VMEM_LIMIT = 56 * 1024 * 1024


def split_index(index):
    return index >> 8, index & (LO - 1)


def one_hot(lo):
    rows = lax.broadcasted_iota(jnp.int32, (LO, lo.shape[1]), 0).astype(BF)
    return jnp.where(rows == lo.astype(BF), jnp.array(1, BF), jnp.array(0, BF))


def pick(blocks, index):
    count, channels, _ = blocks.shape
    hi, lo = split_index(index)
    found = jnp.dot(
        blocks.reshape(count * channels, LO), one_hot(lo), preferred_element_type=F32
    ).reshape(count, channels, index.shape[1])
    got = jnp.zeros((channels, index.shape[1]), F32)
    for h in range(count):
        got = jnp.where(hi == h, found[h], got)
    return got.astype(BF)


def spread(values, index, first, count):
    channels, width = values.shape
    hi, lo = split_index(index)
    parts = [values * jnp.where(hi == first + h, 1.0, 0.0).astype(BF) for h in range(count)]
    wide = jnp.concatenate(parts, axis=0)
    added = lax.dot_general(
        wide, one_hot(lo), (((1,), (1,)), ((), ())), preferred_element_type=F32
    )
    return added.reshape(count, channels, LO)


def whole(array_or_shape):
    shape = array_or_shape.shape
    return pl.BlockSpec(shape, lambda *_: (0,) * len(shape))


def params():
    return pltpu.CompilerParams(vmem_limit_bytes=VMEM_LIMIT)


def fill_blocks(blocks, own_ref, *rest):
    count = own_ref.shape[1] // LO
    for h in range(count):
        blocks[h] = own_ref[:, h * LO : (h + 1) * LO]
    at = count
    for ref in rest:
        blocks[at : at + ref.shape[0]] = ref[...]
        at += ref.shape[0]


def pick_kernel(*refs):
    index_ref, out_ref, blocks = refs[-3], refs[-2], refs[-1]
    fill_blocks(blocks, *refs[:-3])
    for b in range(out_ref.shape[0]):
        out_ref[b] = pick(blocks[...], index_ref[:, b * LO : (b + 1) * LO])


def pick_blocks(own, rest, index):
    channels, slots = own.shape
    width = index.shape[0]
    count = slots // LO + sum(r.shape[0] for r in rest)
    return pl.pallas_call(
        pick_kernel,
        out_shape=jax.ShapeDtypeStruct((width // LO, channels, LO), BF),
        scratch_shapes=[pltpu.VMEM((count, channels, LO), BF)],
        compiler_params=params(),
        name="pick_columns",
    )(own, *rest, index.reshape(1, width))


def conv_kernel(own_ref, z_ref, xy_ref, wt_ref, index_ref, up_ref, out_ref, wg_ref, blocks, got):
    k = pl.program_id(0)
    channels, slots = own_ref.shape

    @pl.when(k == 0)
    def _():
        fill_blocks(blocks, own_ref, z_ref, xy_ref)

    for i in range(GROUP):
        at = k * GROUP + i
        rows = pl.ds(pl.multiple_of(at * channels, 32), channels)
        got[rows, :] = pick(blocks[...], index_ref[pl.ds(at, 1), :])

    @pl.when(k == pl.num_programs(0) - 1)
    def _():
        out_ref[...] = jnp.dot(wt_ref[...], got[...], preferred_element_type=F32).astype(BF)
        term = lax.dot_general(
            up_ref[...], got[...], (((1,), (1,)), ((), ())), preferred_element_type=F32
        )
        height = wg_ref.shape[1]
        for p in range(wg_ref.shape[0]):
            wg_ref[p] = term[p * height : (p + 1) * height]


def convolve(own, z_blocks, xy_blocks, weight_t, index, up, pieces):
    channels, slots = own.shape
    offsets = index.shape[0]
    count = slots // LO + z_blocks.shape[0] + xy_blocks.shape[0]
    flops = 2 * offsets * slots * channels * (count * LO + 2 * channels)
    return pl.pallas_call(
        conv_kernel,
        grid=(offsets // GROUP,),
        in_specs=[
            whole(own),
            whole(z_blocks),
            whole(xy_blocks),
            whole(weight_t),
            whole(index),
            whole(up),
        ],
        out_specs=[
            pl.BlockSpec((channels, slots), lambda k: (0, 0)),
            pl.BlockSpec((pieces, channels // pieces, offsets * channels), lambda k: (0, 0, 0)),
        ],
        out_shape=[
            jax.ShapeDtypeStruct((channels, slots), BF),
            jax.ShapeDtypeStruct((pieces, channels // pieces, offsets * channels), F32),
        ],
        scratch_shapes=[
            pltpu.VMEM((count, channels, LO), BF),
            pltpu.VMEM((offsets * channels, slots), BF),
        ],
        compiler_params=params(),
        cost_estimate=pl.CostEstimate(flops=flops, bytes_accessed=4 << 20, transcendentals=0),
        name="convolve",
    )(own, z_blocks, xy_blocks, weight_t, index, up)


def spread_step(w_ref, index_ref, up_ref, back, first, count, begin):
    k = pl.program_id(0)
    channels = up_ref.shape[0]

    @pl.when(k == 0)
    def _():
        back[...] = jnp.dot(w_ref[...], up_ref[...], preferred_element_type=F32).astype(BF)

    total = None
    for i in range(GROUP):
        at = k * GROUP + i
        rows = pl.ds(pl.multiple_of(at * channels, 32), channels)
        part = spread(back[rows, :], index_ref[pl.ds(begin + at, 1), :], first, count)
        total = part if total is None else total + part
    return total


def spread_kernel(first, begin, w_ref, index_ref, up_ref, *refs):
    acc_ref, back = refs[-2:]
    part = spread_step(w_ref, index_ref, up_ref, back, first, acc_ref.shape[0], begin)

    @pl.when(pl.program_id(0) == 0)
    def _():
        acc_ref[...] = part + refs[0][...] if len(refs) == 3 else part

    @pl.when(pl.program_id(0) > 0)
    def _():
        acc_ref[...] += part


def spread_last_kernel(
    begin, w_ref, index_ref, up_ref, start_ref, ext_ref, z_ref, z_index_ref, out_ref, back, acc
):
    count = acc.shape[0]

    @pl.when(pl.program_id(0) == 0)
    def _():
        acc[...] = start_ref[...] + ext_ref[...] + spread_pairs(z_ref, z_index_ref, count)

    acc[...] += spread_step(w_ref, index_ref, up_ref, back, 0, count, begin)

    @pl.when(pl.program_id(0) == pl.num_programs(0) - 1)
    def _():
        for h in range(count):
            out_ref[:, h * LO : (h + 1) * LO] = acc[h]


def spread_specs(weight, index, up, begin, end):
    channels, slots = up.shape
    steps = end - begin
    return [
        pl.BlockSpec((steps * channels, channels), lambda k: (0, 0)),
        whole(index),
        whole(up),
    ]


def spread_cost(up, count, steps):
    channels, slots = up.shape
    flops = 2 * steps * slots * channels * (count * LO + channels)
    return pl.CostEstimate(flops=flops, bytes_accessed=2 << 20, transcendentals=0)


def weight_rows(weight, begin, end):
    return weight[begin:end].reshape(-1, weight.shape[2])


def spread_grads(weight, index, up, first, count, begin, end, start=None):
    channels, slots = up.shape
    extra = () if start is None else (start,)
    steps = end - begin
    return pl.pallas_call(
        functools.partial(spread_kernel, first, begin),
        grid=(steps // GROUP,),
        in_specs=spread_specs(weight, index, up, begin, end) + [whole(e) for e in extra],
        out_specs=pl.BlockSpec((count, channels, LO), lambda k: (0, 0, 0)),
        out_shape=jax.ShapeDtypeStruct((count, channels, LO), F32),
        scratch_shapes=[pltpu.VMEM((steps * channels, slots), BF)],
        compiler_params=params(),
        cost_estimate=spread_cost(up, count, steps),
        name="spread_grads",
    )(weight_rows(weight, begin, end), index, up, *extra)


def spread_last(weight, index, up, begin, end, start, ext, z_pairs, z_index):
    count, channels, _ = start.shape
    slots = up.shape[1]
    steps = end - begin
    return pl.pallas_call(
        functools.partial(spread_last_kernel, begin),
        grid=(steps // GROUP,),
        in_specs=spread_specs(weight, index, up, begin, end)
        + [
            whole(start),
            pl.BlockSpec(start.shape, lambda k: (0, 0, 0)),
            whole(z_pairs),
            pl.BlockSpec((1, z_index.shape[0]), lambda k: (0, 0)),
        ],
        out_specs=pl.BlockSpec((channels, slots), lambda k: (0, 0)),
        out_shape=jax.ShapeDtypeStruct((channels, slots), F32),
        scratch_shapes=[
            pltpu.VMEM((steps * channels, slots), BF),
            pltpu.VMEM((count, channels, LO), F32),
        ],
        compiler_params=params(),
        cost_estimate=spread_cost(up, count, steps),
        name="spread_last",
    )(weight_rows(weight, begin, end), index, up, start, ext, z_pairs, z_index.reshape(1, -1))


def split_pair(value):
    high = value.astype(BF)
    low = (value - high.astype(F32)).astype(BF)
    return jnp.concatenate([high, low], axis=1)


def spread_pairs(pairs_ref, index_ref, count):
    channels = pairs_ref.shape[1] // 2
    index = jnp.concatenate([index_ref[...], index_ref[...]], axis=1)
    blocks = range(pairs_ref.shape[0])
    values = [pairs_ref[b, :channels, :] for b in blocks] + [
        pairs_ref[b, channels:, :] for b in blocks
    ]
    return spread(jnp.concatenate(values, axis=1), index, 0, count)


def halo_add_kernel(slots, pairs_ref, index_ref, halo_ref, ext_ref, z_ref):
    own_count = slots // LO
    z_count, channels, _ = z_ref.shape[0], ext_ref.shape[1], LO
    part = spread_pairs(pairs_ref, index_ref, own_count + z_count)
    ext_ref[...] = part[:own_count]
    z_ref[...] = split_pair(part[own_count:] + halo_ref[:z_count])


def halo_add(pairs, index, halo, own_count, z_count):
    channels = halo.shape[1]
    return pl.pallas_call(
        functools.partial(halo_add_kernel, own_count * LO),
        out_shape=[
            jax.ShapeDtypeStruct((own_count, channels, LO), F32),
            jax.ShapeDtypeStruct((z_count, 2 * channels, LO), BF),
        ],
        compiler_params=params(),
        name="halo_add",
    )(pairs, index.reshape(1, -1), halo)


def exchange(blocks, peers, per_peer):
    count, channels, _ = blocks.shape
    if per_peer != LO:
        flat = blocks.transpose(1, 0, 2).reshape(channels, peers, per_peer).transpose(1, 0, 2)
    else:
        flat = blocks
    got = lax.all_to_all(flat, "xy", split_axis=0, concat_axis=0, tiled=True)
    if per_peer != LO:
        got = got.transpose(1, 0, 2).reshape(channels, count, LO).transpose(1, 0, 2)
    return got


def shift_z(low_bound, high_bound):
    count = lax.axis_size("gz")
    up = [(i, i + 1) for i in range(count - 1)]
    down = [(b, a) for a, b in up]
    return lax.ppermute(high_bound, "gz", up), lax.ppermute(low_bound, "gz", down)


def on_device(features, weight, z_send, xy_send, kernel_map, cotangent):
    channels, slots = features.shape
    offsets = weight.shape[0]
    peers = lax.axis_size("xy")
    z_list, xy_list = z_send.reshape(-1), xy_send.reshape(-1)
    z_count = z_list.shape[0] // LO
    rim = z_count // 2
    xy_count = xy_list.shape[0] // LO
    per_peer = xy_list.shape[0] // peers
    own_count = slots // LO
    ext_count = own_count + z_count
    index = kernel_map

    outgoing = pick_blocks(features, (), z_list)
    below, above = shift_z(outgoing[:rim], outgoing[rim:])
    z_blocks = jnp.concatenate([below, above], axis=0)

    cotangent, outgoing = lax.optimization_barrier((cotangent, outgoing))
    halo_grad = spread_grads(
        weight, index, cotangent, own_count, z_count + xy_count, 0, offsets
    )
    z_blocks, halo_grad = lax.optimization_barrier((z_blocks, halo_grad))

    sends = pick_blocks(features, (z_blocks,), xy_list)
    both = jnp.concatenate([sends, split_pair(halo_grad[z_count:])], axis=1)
    got = exchange(both, peers, per_peer)
    own_grad = spread_grads(weight, index, cotangent, 0, own_count, 0, offsets // 3)

    xy_blocks, xy_pairs = got[:, :channels], got[:, channels:]
    ext_grad, z_pairs = halo_add(xy_pairs, xy_list, halo_grad, own_count, z_count)
    back_low, back_high = shift_z(z_pairs[:rim], z_pairs[rim:])
    z_back = jnp.concatenate([back_low, back_high], axis=0)

    weight_t = weight.transpose(2, 0, 1).reshape(channels, offsets * channels)
    xy_blocks, own_grad = lax.optimization_barrier((xy_blocks, own_grad))
    layers = lax.axis_size("gz")
    even = channels % (peers * layers) == 0
    out_features, w_term = convolve(
        features,
        z_blocks,
        xy_blocks,
        weight_t,
        index,
        cotangent,
        peers * layers if even else 1,
    )

    w_scale = 1.0 / math.sqrt(slots * peers * layers)
    cotangent, w_term = lax.optimization_barrier((cotangent, w_term))
    middle = 2 * offsets // 3
    own_grad = spread_grads(
        weight, index, cotangent, 0, own_count, offsets // 3, middle, start=own_grad
    )
    if even:
        terms = lax.all_to_all(w_term, ("xy", "gz"), 0, 0, tiled=True)
        own_grad, terms = lax.optimization_barrier((own_grad, terms))
        mine = jnp.sum(terms, axis=0) * w_scale
        spread_out = jnp.broadcast_to(mine, (layers,) + mine.shape)
        rows = lax.all_to_all(spread_out, "gz", 0, 0, tiled=True)
        grad_weight = rows.reshape(-1, rows.shape[2])
    else:
        part = lax.psum_scatter(w_term[0], "xy", scatter_dimension=0, tiled=True)
        grad_weight = lax.psum(part, "gz") * w_scale
    grad_features = spread_last(
        weight, index, cotangent, middle, offsets, own_grad, ext_grad, z_back, z_list
    )
    return (out_features, grad_features, grad_weight)


def solution(mesh):
    slab = P(None, ("parts", "xy", "gz"))
    lists = P(("parts", "xy"), "gz", None)
    return jax.shard_map(
        on_device,
        mesh=mesh,
        in_specs=(slab, P(), lists, lists, slab, slab),
        out_specs=(slab, slab, P(("parts", "xy"), None)),
        check_vma=False,
    )
```

```python
import functools
import math

import jax
import jax.numpy as jnp
from jax import lax
from jax.experimental import pallas as pl
from jax.experimental.pallas import tpu as pltpu
from jax.sharding import PartitionSpec as P

LO = 256
BF = jnp.bfloat16
F32 = jnp.float32
GROUP = 3
VMEM_LIMIT = 56 * 1024 * 1024


def split_index(index):
    return index >> 8, index & (LO - 1)


def one_hot(lo):
    rows = lax.broadcasted_iota(jnp.int32, (LO, lo.shape[1]), 0).astype(BF)
    return jnp.where(rows == lo.astype(BF), jnp.array(1, BF), jnp.array(0, BF))


def pick(blocks, index):
    count, channels, _ = blocks.shape
    hi, lo = split_index(index)
    found = jnp.dot(
        blocks.reshape(count * channels, LO), one_hot(lo), preferred_element_type=F32
    ).reshape(count, channels, index.shape[1])
    got = jnp.zeros((channels, index.shape[1]), F32)
    for h in range(count):
        got = jnp.where(hi == h, found[h], got)
    return got.astype(BF)


def spread(values, index, first, count):
    channels, width = values.shape
    hi, lo = split_index(index)
    parts = [values * jnp.where(hi == first + h, 1.0, 0.0).astype(BF) for h in range(count)]
    wide = jnp.concatenate(parts, axis=0)
    added = lax.dot_general(
        wide, one_hot(lo), (((1,), (1,)), ((), ())), preferred_element_type=F32
    )
    return added.reshape(count, channels, LO)


def whole(array_or_shape):
    shape = array_or_shape.shape
    return pl.BlockSpec(shape, lambda *_: (0,) * len(shape))


def params():
    return pltpu.CompilerParams(vmem_limit_bytes=VMEM_LIMIT)


def fill_blocks(blocks, own_ref, *rest):
    count = own_ref.shape[1] // LO
    for h in range(count):
        blocks[h] = own_ref[:, h * LO : (h + 1) * LO]
    at = count
    for ref in rest:
        blocks[at : at + ref.shape[0]] = ref[...]
        at += ref.shape[0]


def pick_kernel(*refs):
    index_ref, out_ref, blocks = refs[-3], refs[-2], refs[-1]
    fill_blocks(blocks, *refs[:-3])
    for b in range(out_ref.shape[0]):
        out_ref[b] = pick(blocks[...], index_ref[:, b * LO : (b + 1) * LO])


def pick_blocks(own, rest, index):
    channels, slots = own.shape
    width = index.shape[0]
    count = slots // LO + sum(r.shape[0] for r in rest)
    return pl.pallas_call(
        pick_kernel,
        out_shape=jax.ShapeDtypeStruct((width // LO, channels, LO), BF),
        scratch_shapes=[pltpu.VMEM((count, channels, LO), BF)],
        compiler_params=params(),
        name="pick_columns",
    )(own, *rest, index.reshape(1, width))


def conv_kernel(own_ref, z_ref, xy_ref, wt_ref, index_ref, up_ref, out_ref, wg_ref, blocks, got):
    k = pl.program_id(0)
    channels, slots = own_ref.shape

    @pl.when(k == 0)
    def _():
        fill_blocks(blocks, own_ref, z_ref, xy_ref)

    for i in range(GROUP):
        at = k * GROUP + i
        rows = pl.ds(pl.multiple_of(at * channels, 32), channels)
        got[rows, :] = pick(blocks[...], index_ref[pl.ds(at, 1), :])

    @pl.when(k == pl.num_programs(0) - 1)
    def _():
        out_ref[...] = jnp.dot(wt_ref[...], got[...], preferred_element_type=F32).astype(BF)
        term = lax.dot_general(
            up_ref[...], got[...], (((1,), (1,)), ((), ())), preferred_element_type=F32
        )
        height = wg_ref.shape[1]
        for p in range(wg_ref.shape[0]):
            wg_ref[p] = term[p * height : (p + 1) * height]


def convolve(own, z_blocks, xy_blocks, weight_t, index, up, pieces):
    channels, slots = own.shape
    offsets = index.shape[0]
    count = slots // LO + z_blocks.shape[0] + xy_blocks.shape[0]
    flops = 2 * offsets * slots * channels * (count * LO + 2 * channels)
    return pl.pallas_call(
        conv_kernel,
        grid=(offsets // GROUP,),
        in_specs=[
            whole(own),
            whole(z_blocks),
            whole(xy_blocks),
            whole(weight_t),
            whole(index),
            whole(up),
        ],
        out_specs=[
            pl.BlockSpec((channels, slots), lambda k: (0, 0)),
            pl.BlockSpec((pieces, channels // pieces, offsets * channels), lambda k: (0, 0, 0)),
        ],
        out_shape=[
            jax.ShapeDtypeStruct((channels, slots), BF),
            jax.ShapeDtypeStruct((pieces, channels // pieces, offsets * channels), F32),
        ],
        scratch_shapes=[
            pltpu.VMEM((count, channels, LO), BF),
            pltpu.VMEM((offsets * channels, slots), BF),
        ],
        compiler_params=params(),
        cost_estimate=pl.CostEstimate(flops=flops, bytes_accessed=4 << 20, transcendentals=0),
        name="convolve",
    )(own, z_blocks, xy_blocks, weight_t, index, up)


def spread_step(w_ref, index_ref, up_ref, back, first, count, begin):
    k = pl.program_id(0)
    channels = up_ref.shape[0]

    @pl.when(k == 0)
    def _():
        back[...] = jnp.dot(w_ref[...], up_ref[...], preferred_element_type=F32).astype(BF)

    total = None
    for i in range(GROUP):
        at = k * GROUP + i
        rows = pl.ds(pl.multiple_of(at * channels, 32), channels)
        part = spread(back[rows, :], index_ref[pl.ds(begin + at, 1), :], first, count)
        total = part if total is None else total + part
    return total


def spread_kernel(first, begin, w_ref, index_ref, up_ref, *refs):
    acc_ref, back = refs[-2:]
    part = spread_step(w_ref, index_ref, up_ref, back, first, acc_ref.shape[0], begin)

    @pl.when(pl.program_id(0) == 0)
    def _():
        acc_ref[...] = part + refs[0][...] if len(refs) == 3 else part

    @pl.when(pl.program_id(0) > 0)
    def _():
        acc_ref[...] += part


def spread_last_kernel(
    begin, w_ref, index_ref, up_ref, start_ref, ext_ref, z_ref, z_index_ref, out_ref, back, acc
):
    count = acc.shape[0]

    @pl.when(pl.program_id(0) == 0)
    def _():
        acc[...] = start_ref[...] + ext_ref[...] + spread_pairs(z_ref, z_index_ref, count)

    acc[...] += spread_step(w_ref, index_ref, up_ref, back, 0, count, begin)

    @pl.when(pl.program_id(0) == pl.num_programs(0) - 1)
    def _():
        for h in range(count):
            out_ref[:, h * LO : (h + 1) * LO] = acc[h]


def spread_specs(weight, index, up, begin, end):
    channels, slots = up.shape
    steps = end - begin
    return [
        pl.BlockSpec((steps * channels, channels), lambda k: (0, 0)),
        whole(index),
        whole(up),
    ]


def spread_cost(up, count, steps):
    channels, slots = up.shape
    flops = 2 * steps * slots * channels * (count * LO + channels)
    return pl.CostEstimate(flops=flops, bytes_accessed=2 << 20, transcendentals=0)


def weight_rows(weight, begin, end):
    return weight[begin:end].reshape(-1, weight.shape[2])


def spread_grads(weight, index, up, first, count, begin, end, start=None):
    channels, slots = up.shape
    extra = () if start is None else (start,)
    steps = end - begin
    return pl.pallas_call(
        functools.partial(spread_kernel, first, begin),
        grid=(steps // GROUP,),
        in_specs=spread_specs(weight, index, up, begin, end) + [whole(e) for e in extra],
        out_specs=pl.BlockSpec((count, channels, LO), lambda k: (0, 0, 0)),
        out_shape=jax.ShapeDtypeStruct((count, channels, LO), F32),
        scratch_shapes=[pltpu.VMEM((steps * channels, slots), BF)],
        compiler_params=params(),
        cost_estimate=spread_cost(up, count, steps),
        name="spread_grads",
    )(weight_rows(weight, begin, end), index, up, *extra)


def spread_last(weight, index, up, begin, end, start, ext, z_pairs, z_index):
    count, channels, _ = start.shape
    slots = up.shape[1]
    steps = end - begin
    return pl.pallas_call(
        functools.partial(spread_last_kernel, begin),
        grid=(steps // GROUP,),
        in_specs=spread_specs(weight, index, up, begin, end)
        + [
            whole(start),
            pl.BlockSpec(start.shape, lambda k: (0, 0, 0)),
            whole(z_pairs),
            pl.BlockSpec((1, z_index.shape[0]), lambda k: (0, 0)),
        ],
        out_specs=pl.BlockSpec((channels, slots), lambda k: (0, 0)),
        out_shape=jax.ShapeDtypeStruct((channels, slots), F32),
        scratch_shapes=[
            pltpu.VMEM((steps * channels, slots), BF),
            pltpu.VMEM((count, channels, LO), F32),
        ],
        compiler_params=params(),
        cost_estimate=spread_cost(up, count, steps),
        name="spread_last",
    )(weight_rows(weight, begin, end), index, up, start, ext, z_pairs, z_index.reshape(1, -1))


def split_pair(value):
    high = value.astype(BF)
    low = (value - high.astype(F32)).astype(BF)
    return jnp.concatenate([high, low], axis=1)


def spread_pairs(pairs_ref, index_ref, count):
    channels = pairs_ref.shape[1] // 2
    index = jnp.concatenate([index_ref[...], index_ref[...]], axis=1)
    blocks = range(pairs_ref.shape[0])
    values = [pairs_ref[b, :channels, :] for b in blocks] + [
        pairs_ref[b, channels:, :] for b in blocks
    ]
    return spread(jnp.concatenate(values, axis=1), index, 0, count)


def halo_add_kernel(slots, pairs_ref, index_ref, halo_ref, ext_ref, z_ref):
    own_count = slots // LO
    z_count, channels, _ = z_ref.shape[0], ext_ref.shape[1], LO
    part = spread_pairs(pairs_ref, index_ref, own_count + z_count)
    ext_ref[...] = part[:own_count]
    z_ref[...] = split_pair(part[own_count:] + halo_ref[:z_count])


def halo_add(pairs, index, halo, own_count, z_count):
    channels = halo.shape[1]
    return pl.pallas_call(
        functools.partial(halo_add_kernel, own_count * LO),
        out_shape=[
            jax.ShapeDtypeStruct((own_count, channels, LO), F32),
            jax.ShapeDtypeStruct((z_count, 2 * channels, LO), BF),
        ],
        compiler_params=params(),
        name="halo_add",
    )(pairs, index.reshape(1, -1), halo)


def exchange(blocks, peers, per_peer):
    count, channels, _ = blocks.shape
    if per_peer != LO:
        flat = blocks.transpose(1, 0, 2).reshape(channels, peers, per_peer).transpose(1, 0, 2)
    else:
        flat = blocks
    got = lax.all_to_all(flat, "xy", split_axis=0, concat_axis=0, tiled=True)
    if per_peer != LO:
        got = got.transpose(1, 0, 2).reshape(channels, count, LO).transpose(1, 0, 2)
    return got


def shift_z(low_bound, high_bound):
    count = lax.axis_size("gz")
    up = [(i, i + 1) for i in range(count - 1)]
    down = [(b, a) for a, b in up]
    return lax.ppermute(high_bound, "gz", up), lax.ppermute(low_bound, "gz", down)


def on_device(features, weight, z_send, xy_send, kernel_map, cotangent):
    channels, slots = features.shape
    offsets = weight.shape[0]
    peers = lax.axis_size("xy")
    z_list, xy_list = z_send.reshape(-1), xy_send.reshape(-1)
    z_count = z_list.shape[0] // LO
    rim = z_count // 2
    xy_count = xy_list.shape[0] // LO
    per_peer = xy_list.shape[0] // peers
    own_count = slots // LO
    ext_count = own_count + z_count
    index = kernel_map

    outgoing = pick_blocks(features, (), z_list)
    below, above = shift_z(outgoing[:rim], outgoing[rim:])
    z_blocks = jnp.concatenate([below, above], axis=0)

    cotangent, outgoing = lax.optimization_barrier((cotangent, outgoing))
    halo_grad = spread_grads(
        weight, index, cotangent, own_count, z_count + xy_count, 0, offsets
    )
    z_blocks, halo_grad = lax.optimization_barrier((z_blocks, halo_grad))

    sends = pick_blocks(features, (z_blocks,), xy_list)
    both = jnp.concatenate([sends, split_pair(halo_grad[z_count:])], axis=1)
    got = exchange(both, peers, per_peer)
    own_grad = spread_grads(weight, index, cotangent, 0, own_count, 0, offsets // 3)

    xy_blocks, xy_pairs = got[:, :channels], got[:, channels:]
    ext_grad, z_pairs = halo_add(xy_pairs, xy_list, halo_grad, own_count, z_count)
    back_low, back_high = shift_z(z_pairs[:rim], z_pairs[rim:])
    z_back = jnp.concatenate([back_low, back_high], axis=0)

    weight_t = weight.transpose(2, 0, 1).reshape(channels, offsets * channels)
    xy_blocks, own_grad = lax.optimization_barrier((xy_blocks, own_grad))
    layers = lax.axis_size("gz")
    even = channels % (peers * layers) == 0
    out_features, w_term = convolve(
        features,
        z_blocks,
        xy_blocks,
        weight_t,
        index,
        cotangent,
        peers * layers if even else 1,
    )

    w_scale = 1.0 / math.sqrt(slots * peers * layers)
    cotangent, w_term = lax.optimization_barrier((cotangent, w_term))
    middle = offsets - GROUP
    own_grad = spread_grads(
        weight, index, cotangent, 0, own_count, offsets // 3, middle, start=own_grad
    )
    if even:
        terms = lax.all_to_all(w_term, ("xy", "gz"), 0, 0, tiled=True)
        own_grad, terms = lax.optimization_barrier((own_grad, terms))
        mine = jnp.sum(terms, axis=0) * w_scale
        spread_out = jnp.broadcast_to(mine, (layers,) + mine.shape)
        rows = lax.all_to_all(spread_out, "gz", 0, 0, tiled=True)
        grad_weight = rows.reshape(-1, rows.shape[2])
    else:
        part = lax.psum_scatter(w_term[0], "xy", scatter_dimension=0, tiled=True)
        grad_weight = lax.psum(part, "gz") * w_scale
    grad_features = spread_last(
        weight, index, cotangent, middle, offsets, own_grad, ext_grad, z_back, z_list
    )
    return (out_features, grad_features, grad_weight)


def solution(mesh):
    slab = P(None, ("parts", "xy", "gz"))
    lists = P(("parts", "xy"), "gz", None)
    return jax.shard_map(
        on_device,
        mesh=mesh,
        in_specs=(slab, P(), lists, lists, slab, slab),
        out_specs=(slab, slab, P(("parts", "xy"), None)),
        check_vma=False,
    )
```
